256 devices in a mesh: gx: 8 (over y, z_lo), gy: 8 (over x, core), gz: 4 (over z_hi).
Axes of the slice: x: 4, y: 4, z: 8 (z_hi: 4, z_lo: 2; z = z_hi * 2 + z_lo), core: 2. Of those that a mesh axis runs over, the one named last changes fastest.
Arguments:
- coefficients: bfloat16 [262144, 16, 128], P(('gx', 'gy', 'gz')), may hold values from -6 to 6
- translations: bfloat16 [4, 2, 2, 128, 128], replicated, may hold values from -0.375 to 0.375
- box_gains: bfloat16 [4, 262144, 128], P(None, ('gx', 'gy', 'gz')), may hold values from 0.25 to 1.75
Outputs:
- result: bfloat16 [262144, 16, 128], P(('gx', 'gy', 'gz'))
The draws below stay inside these ranges and needn't reach their ends.
All inputs are finite; a program needn't handle non-finite values.
Results may differ from the reference program's by a relative error of at most 0.0064.
Values may be sent and summed in bfloat16 or wider, within the bound.
A program may use at most 128 MiB of HBM per device.

```python
import jax
import jax.numpy as jnp
from jax import lax

COEFS = 128
VECS = 16
LEVELS = 4
BOX_DEV = 1024
BOXES = 262144
N_GX = 8
N_GY = 8
N_GZ = 4


def steps_of(key, dims, pieces, least, high):
    def one(axis_at, blocks):
        steps = jax.random.uniform(jax.random.fold_in(jax.random.fold_in(key, 6), axis_at), (blocks,), jnp.float32, least / len(pieces), high / len(pieces))
        return jnp.repeat(jnp.exp(steps), dims[axis_at] // blocks).reshape((-1,) + (1,) * (len(dims) - axis_at - 1))

    factor_of = one(*pieces[0])
    for cut in pieces[1:]:
        factor_of = factor_of * one(*cut)
    return factor_of


def scatter_about(stream_key, shape, deviation, limit, split=(), dtype=jnp.bfloat16):
    values = jax.random.normal(stream_key, shape, jnp.float32) * deviation
    if len(split) > 0:
        values = steps_of(stream_key, shape, split, -0.22, 0.18) * values
    return jnp.clip(values, min=-limit, max=limit).astype(dtype)


def setup_inputs(seed: int = 0) -> dict:
    streams_of = jax.random.split(jax.random.key(seed), 4)
    return {
        "coefficients": scatter_about(streams_of[0], (BOXES, VECS, COEFS), 1.0, 6.0, ((0, 256),)),
        "translations": scatter_about(streams_of[1], (LEVELS, 2, 2, COEFS, COEFS), (2 * COEFS) ** -0.5, 0.375),
        "box_gains": jnp.clip(1.0 + 0.15 * jax.random.normal(streams_of[2], (LEVELS, BOXES, COEFS), jnp.float32), 0.25, 1.75).astype(jnp.bfloat16),
    }


def apply_level(coefficients, block_matrices, level_gains, bit_place):
    total_blocks = N_GX * N_GY * N_GZ
    span_count = 2 ** bit_place
    outer_count = total_blocks // (2 * span_count)
    half_rows = BOX_DEV // 2
    shaped = coefficients.reshape(outer_count, 2, span_count, 2, half_rows, VECS, COEFS)
    gain_shaped = level_gains.reshape(outer_count, 2, span_count, 2, half_rows, COEFS)

    def single(item_pair):
        item_block, gain_block = item_pair
        combined = jnp.einsum('vcsjrk,tvkm->sctjrm', item_block.astype(jnp.float32), block_matrices.astype(jnp.float32))
        return (combined * gain_block[:, :, :, :, None, :].astype(jnp.float32)).astype(jnp.bfloat16)

    produced = lax.map(single, (shaped, gain_shaped))
    return produced.reshape(BOXES, VECS, COEFS)


def reference(coefficients, translations, box_gains):
    places = [(N_GY * N_GZ).bit_length() - 1, 0, 1, 2]
    current = coefficients
    for section_index in range(LEVELS):
        current = apply_level(current, translations[section_index], box_gains[section_index], places[section_index])
    return current
```

```python
import functools

import jax
import jax.numpy as jnp
from jax import lax
from jax.experimental import pallas as pl
from jax.experimental.pallas import tpu as pltpu
from jax.sharding import PartitionSpec as P

MESH = pl.DeviceIdType.MESH
LEVELS = 4
CHUNKS = 16
AHEAD = 3
LAGS = (0, 2, 4, 5)


def butterfly(
    coefs, blocks, gains, result,
    own, blocks_in, weights, factors, kept, given, arrived, done,
    own_sems, block_sem, gain_sems, send_sems, recv_sems, out_sems,
):
    gx, gy, gz = lax.axis_index("gx"), lax.axis_index("gy"), lax.axis_index("gz")
    sides = (gx % 2, gz % 2, gz // 2, gy % 2)
    partners = (
        {"gx": gx + 1 - 2 * sides[0]},
        {"gz": gz + 1 - 2 * sides[1]},
        {"gz": gz + 2 - 4 * sides[2]},
        {"gy": gy + 1 - 2 * sides[3]},
    )
    half, vecs, width = own.shape
    size = half // CHUNKS
    rows = size * vecs

    def part(chunk):
        return pl.ds(chunk * size, size)

    def targets(level):
        if level == LEVELS - 1:
            return (0, 1)
        return (1 - sides[level + 1], sides[level + 1])

    def load_own(chunk):
        return pltpu.make_async_copy(
            coefs.at[sides[0], part(chunk)], own.at[part(chunk)], own_sems.at[chunk]
        )

    def load_gains(level, place):
        return pltpu.make_async_copy(
            gains.at[level, targets(level)[place]], factors.at[level, place], gain_sems.at[level, place]
        )

    def exchange(level, chunk):
        if level == 0:
            source = coefs.at[1 - sides[0], part(chunk)]
        else:
            source = given.at[level - 1, part(chunk)]
        return pltpu.make_async_remote_copy(
            src_ref=source,
            dst_ref=arrived.at[level, part(chunk)],
            send_sem=send_sems.at[level, chunk],
            recv_sem=recv_sems.at[level, chunk],
            device_id=partners[level],
            device_id_type=MESH,
        )

    def store(place, chunk):
        return pltpu.make_async_copy(
            done.at[place, part(chunk)], result.at[place, part(chunk)], out_sems.at[place, chunk]
        )

    block_copy = pltpu.make_async_copy(blocks, blocks_in, block_sem)
    block_copy.start()
    for chunk in range(CHUNKS):
        load_own(chunk).start()
    for level in range(LEVELS):
        for place in range(2):
            load_gains(level, place).start()

    barrier = pltpu.get_barrier_semaphore()
    for level in range(LEVELS):
        pl.semaphore_signal(barrier, inc=1, device_id=partners[level], device_id_type=MESH)
    pl.semaphore_wait(barrier, LEVELS)

    for chunk in range(AHEAD):
        exchange(0, chunk).start()

    block_copy.wait()
    for level in range(LEVELS):
        for place in range(2):
            for origin in range(2):
                source = sides[level] if origin == 0 else 1 - sides[level]
                weights[level, pl.ds(origin * width, width), pl.ds(place * width, width)] = blocks_in[
                    level, targets(level)[place], source
                ]
    for level in range(LEVELS):
        for place in range(2):
            load_gains(level, place).wait()

    def work(level, chunk):
        here = part(chunk)
        if level == 0:
            load_own(chunk).wait()
            self_rows = own
        else:
            self_rows = kept.at[level - 1]
        exchange(level, chunk).wait_recv()
        joined = jnp.concatenate(
            [self_rows[here].reshape(rows, width), arrived[level, here].reshape(rows, width)], axis=1
        )
        total = jnp.dot(joined, weights[level], preferred_element_type=jnp.float32)
        for place in range(2):
            scale = factors[level, place, here].astype(jnp.float32)
            columns = total[:, place * width : (place + 1) * width].reshape(size, vecs, width)
            values = (columns * scale[:, None, :]).astype(jnp.bfloat16)
            if level == LEVELS - 1:
                done[place, here] = values
                store(place, chunk).start()
            elif place == 0:
                given[level, here] = values
                exchange(level + 1, chunk).start()
            else:
                kept[level, here] = values

    def step(index, carry):
        for level in range(LEVELS):
            chunk = index - LAGS[level]

            @pl.when((chunk >= 0) & (chunk < CHUNKS))
            def _(level=level, chunk=chunk):
                work(level, chunk)

            if level == 0:

                @pl.when(index + AHEAD < CHUNKS)
                def _():
                    exchange(0, index + AHEAD).start()

        return carry

    lax.fori_loop(0, CHUNKS + LAGS[-1], step, 0)

    def finish(chunk, carry):
        for level in range(LEVELS):
            exchange(level, chunk).wait_send()
        for place in range(2):
            store(place, chunk).wait()
        return carry

    lax.fori_loop(0, CHUNKS, finish, 0)


def shards(coefficients, translations, box_gains):
    boxes, vecs, width = coefficients.shape
    half = boxes // 2
    bf16 = jnp.bfloat16
    anywhere = pl.BlockSpec(memory_space=pl.ANY)
    result = pl.pallas_call(
        butterfly,
        out_shape=jax.ShapeDtypeStruct((2, half, vecs, width), bf16),
        in_specs=[anywhere] * 3,
        out_specs=anywhere,
        scratch_shapes=[
            pltpu.VMEM((half, vecs, width), bf16),
            pltpu.VMEM(translations.shape, bf16),
            pltpu.VMEM((LEVELS, 2 * width, 2 * width), bf16),
            pltpu.VMEM((LEVELS, 2, half, width), bf16),
            pltpu.VMEM((LEVELS - 1, half, vecs, width), bf16),
            pltpu.VMEM((LEVELS - 1, half, vecs, width), bf16),
            pltpu.VMEM((LEVELS, half, vecs, width), bf16),
            pltpu.VMEM((2, half, vecs, width), bf16),
            pltpu.SemaphoreType.DMA((CHUNKS,)),
            pltpu.SemaphoreType.DMA,
            pltpu.SemaphoreType.DMA((LEVELS, 2)),
            pltpu.SemaphoreType.DMA((LEVELS, CHUNKS)),
            pltpu.SemaphoreType.DMA((LEVELS, CHUNKS)),
            pltpu.SemaphoreType.DMA((2, CHUNKS)),
        ],
        compiler_params=pltpu.CompilerParams(
            collective_id=0, has_side_effects=True, vmem_limit_bytes=48 * 2**20
        ),
        cost_estimate=pl.CostEstimate(
            flops=LEVELS * 2 * half * vecs * 4 * width * width,
            bytes_accessed=10 * 2**20,
            transcendentals=0,
        ),
    )(
        coefficients.reshape(2, half, vecs, width),
        translations,
        box_gains.reshape(LEVELS, 2, half, width),
    )
    return result.reshape(boxes, vecs, width)


def solution(mesh):
    return jax.shard_map(
        shards,
        mesh=mesh,
        in_specs=(P(("gx", "gy", "gz"), None, None), P(), P(None, ("gx", "gy", "gz"), None)),
        out_specs=P(("gx", "gy", "gz"), None, None),
        check_vma=False,
    )
```

```python
import functools

import jax
import jax.numpy as jnp
from jax import lax
from jax.experimental import pallas as pl
from jax.experimental.pallas import tpu as pltpu
from jax.sharding import PartitionSpec as P

MESH = pl.DeviceIdType.MESH
LEVELS = 4
SMALL = 16
LARGE = 32
HEAD = 2
TAIL = 2
FIRST = 2
AHEAD = 2
LAGS = (0, 2, 7, 9)
PASS_LAG = 4


def butterfly(
    coefs, blocks, gains, result,
    own, blocks_in, weights, factors, kept, given, arrived, passing,
    own_sem, block_sem, gain_sem, send_sems, recv_sems, pass_sems,
):
    gx, gy, gz = lax.axis_index("gx"), lax.axis_index("gy"), lax.axis_index("gz")
    sides = (gx % 2, gz % 2, gz // 2, gy % 2)
    partners = (
        {"gx": gx + 1 - 2 * sides[0]},
        {"gz": gz + 1 - 2 * sides[1]},
        {"gz": (gz + 1 + 2 * sides[3]) % 4},
        {"gy": gy + 1 - 2 * sides[3]},
    )
    half, vecs, width = own.shape
    larges = (half - (HEAD + TAIL) * SMALL) // LARGE
    chunks = larges + HEAD + TAIL

    def part(chunk, size):
        if size == LARGE:
            return pl.ds((chunk - HEAD) * LARGE + HEAD * SMALL, LARGE)
        late = (chunk + chunks - larges - HEAD) // chunks
        return pl.ds(chunk * SMALL + late * larges * (LARGE - SMALL), SMALL)

    def by_size(chunk, action):
        inner = (chunk >= HEAD) & (chunk < HEAD + larges)

        @pl.when(inner)
        def _():
            action(chunk, LARGE)

        @pl.when(jnp.logical_not(inner))
        def _():
            action(chunk, SMALL)

    def targets(level):
        if level == LEVELS - 1:
            return (0, 1)
        return (1 - sides[level + 1], sides[level + 1])

    def load_gains(level, place):
        return pltpu.make_async_copy(
            gains.at[level, targets(level)[place]], factors.at[level, place], gain_sem
        )

    def exchange(level, chunk, size):
        if level == 0:
            source = coefs.at[1 - sides[0], part(chunk, size)]
        else:
            source = given.at[level - 1, part(chunk, size)]
        return pltpu.make_async_remote_copy(
            src_ref=source,
            dst_ref=passing.at[part(chunk, size)] if level == 2 else arrived.at[level, part(chunk, size)],
            send_sem=send_sems.at[level],
            recv_sem=pass_sems.at[chunk] if level == 2 else recv_sems.at[level, chunk],
            device_id=partners[level],
            device_id_type=MESH,
        )

    def onward(chunk, size):
        return pltpu.make_async_remote_copy(
            src_ref=passing.at[part(chunk, size)],
            dst_ref=arrived.at[2, part(chunk, size)],
            send_sem=send_sems.at[LEVELS],
            recv_sem=recv_sems.at[2, chunk],
            device_id=partners[2],
            device_id_type=MESH,
        )

    own_copy = pltpu.make_async_copy(coefs.at[sides[0]], own, own_sem)
    block_copy = pltpu.make_async_copy(blocks, blocks_in, block_sem)
    block_copy.start()
    own_copy.start()
    for level in range(LEVELS):
        for place in range(2):
            load_gains(level, place).start()

    barrier = pltpu.get_barrier_semaphore()
    for peer in (partners[0], {"gz": (gz + 1) % 4}, {"gz": (gz + 3) % 4}, partners[3]):
        pl.semaphore_signal(barrier, inc=1, device_id=peer, device_id_type=MESH)
    pl.semaphore_wait(barrier, 4)

    for chunk in range(FIRST):
        exchange(0, chunk, SMALL if chunk < HEAD else LARGE).start()

    block_copy.wait()
    for level in range(LEVELS):
        for place in range(2):
            for origin in range(2):
                source = sides[level] if origin == 0 else 1 - sides[level]
                weights[level, pl.ds(origin * width, width), pl.ds(place * width, width)] = blocks_in[
                    level, targets(level)[place], source
                ]
    pltpu.make_async_copy(factors, factors, gain_sem).wait()
    own_copy.wait()

    def work(level, chunk, size):
        here = part(chunk, size)
        rows = size * vecs
        if level == 0:
            self_rows = own
        else:
            self_rows = kept.at[level - 1]
        if level == 2:
            onward(chunk, size).wait_recv()
        else:
            exchange(level, chunk, size).wait_recv()
        joined = jnp.concatenate(
            [self_rows[here].reshape(rows, width), arrived[level, here].reshape(rows, width)], axis=1
        )
        total = jnp.dot(joined, weights[level], preferred_element_type=jnp.float32)
        for place in range(2):
            scale = factors[level, place, here].astype(jnp.float32)
            columns = total[:, place * width : (place + 1) * width].reshape(size, vecs, width)
            values = (columns * scale[:, None, :]).astype(jnp.bfloat16)
            if level == LEVELS - 1:
                result[place, here] = values
            elif place == 0:
                given[level, here] = values
                exchange(level + 1, chunk, size).start()
            else:
                kept[level, here] = values

    def forward(chunk, size):
        exchange(2, chunk, size).wait_recv()
        onward(chunk, size).start()

    def when_valid(chunk, action):
        @pl.when((chunk >= 0) & (chunk < chunks))
        def _():
            by_size(chunk, action)

    def begin(chunk, size):
        exchange(0, chunk, size).start()

    def step(index, carry):
        when_valid(index, functools.partial(work, 0))
        if FIRST < AHEAD + 1:

            @pl.when(index == 0)
            def _():
                for chunk in range(FIRST, AHEAD):
                    begin(chunk, SMALL if chunk < HEAD else LARGE)

        when_valid(index + AHEAD, begin)
        when_valid(index - LAGS[1], functools.partial(work, 1))
        when_valid(index - PASS_LAG, forward)
        when_valid(index - LAGS[2], functools.partial(work, 2))
        when_valid(index - LAGS[3], functools.partial(work, 3))
        return carry

    lax.fori_loop(0, chunks + LAGS[-1], step, 0)

    for index in range(LEVELS + 1):
        pltpu.make_async_copy(arrived.at[0], arrived.at[0], send_sems.at[index]).wait()


def in_hbm(array):
    return pltpu.with_memory_space_constraint(array, pltpu.HBM)


def shards(coefficients, translations, box_gains):
    boxes, vecs, width = coefficients.shape
    half = boxes // 2
    chunks = (half - (HEAD + TAIL) * SMALL) // LARGE + HEAD + TAIL
    bf16 = jnp.bfloat16
    anywhere = pl.BlockSpec(memory_space=pltpu.HBM)
    result = pl.pallas_call(
        butterfly,
        out_shape=pltpu.VMEM((2, half, vecs, width), bf16),
        in_specs=[anywhere] * 3,
        out_specs=pl.BlockSpec(memory_space=pltpu.VMEM),
        scratch_shapes=[
            pltpu.VMEM((half, vecs, width), bf16),
            pltpu.VMEM(translations.shape, bf16),
            pltpu.VMEM((LEVELS, 2 * width, 2 * width), bf16),
            pltpu.VMEM((LEVELS, 2, half, width), bf16),
            pltpu.VMEM((LEVELS - 1, half, vecs, width), bf16),
            pltpu.VMEM((LEVELS - 1, half, vecs, width), bf16),
            pltpu.VMEM((LEVELS, half, vecs, width), bf16),
            pltpu.VMEM((half, vecs, width), bf16),
            pltpu.SemaphoreType.DMA,
            pltpu.SemaphoreType.DMA,
            pltpu.SemaphoreType.DMA,
            pltpu.SemaphoreType.DMA((LEVELS + 1,)),
            pltpu.SemaphoreType.DMA((LEVELS, chunks)),
            pltpu.SemaphoreType.DMA((chunks,)),
        ],
        compiler_params=pltpu.CompilerParams(
            collective_id=0, has_side_effects=True, vmem_limit_bytes=48 * 2**20
        ),
        cost_estimate=pl.CostEstimate(
            flops=LEVELS * 2 * half * vecs * 4 * width * width,
            bytes_accessed=10 * 2**20,
            transcendentals=0,
        ),
    )(
        in_hbm(coefficients.reshape(2, half, vecs, width)),
        in_hbm(translations),
        in_hbm(box_gains.reshape(LEVELS, 2, half, width)),
    )
    return result.reshape(boxes, vecs, width)


def solution(mesh):
    return jax.shard_map(
        shards,
        mesh=mesh,
        in_specs=(P(("gx", "gy", "gz"), None, None), P(), P(None, ("gx", "gy", "gz"), None)),
        out_specs=P(("gx", "gy", "gz"), None, None),
        check_vma=False,
    )
```

```python
import functools

import jax
import jax.numpy as jnp
from jax import lax
from jax.experimental import pallas as pl
from jax.experimental.pallas import tpu as pltpu
from jax.sharding import PartitionSpec as P

MESH = pl.DeviceIdType.MESH
LEVELS = 4
SMALL = 16
LARGE = 32
HEAD = 6
TAIL = 2
FIRST = 2
AHEAD = 3
LAGS = (0, 2, 9, 11)
PASS_LAG = 5


def butterfly(
    coefs, blocks, gains, result,
    own, blocks_in, weights, factors, kept, given, arrived, passing,
    own_sem, block_sem, gain_sem, send_sems, recv_sems, pass_sems,
):
    gx, gy, gz = lax.axis_index("gx"), lax.axis_index("gy"), lax.axis_index("gz")
    sides = (gx % 2, gz % 2, gz // 2, gy % 2)
    partners = (
        {"gx": gx + 1 - 2 * sides[0]},
        {"gz": gz + 1 - 2 * sides[1]},
        {"gz": (gz + 1 + 2 * sides[3]) % 4},
        {"gy": gy + 1 - 2 * sides[3]},
    )
    half, vecs, width = own.shape
    larges = (half - (HEAD + TAIL) * SMALL) // LARGE
    chunks = larges + HEAD + TAIL

    def part(chunk, size):
        if size == LARGE:
            return pl.ds((chunk - HEAD) * LARGE + HEAD * SMALL, LARGE)
        late = (chunk + chunks - larges - HEAD) // chunks
        return pl.ds(chunk * SMALL + late * larges * (LARGE - SMALL), SMALL)

    def by_size(chunk, action):
        inner = (chunk >= HEAD) & (chunk < HEAD + larges)

        @pl.when(inner)
        def _():
            action(chunk, LARGE)

        @pl.when(jnp.logical_not(inner))
        def _():
            action(chunk, SMALL)

    def targets(level):
        if level == LEVELS - 1:
            return (0, 1)
        return (1 - sides[level + 1], sides[level + 1])

    def load_gains(level, place):
        return pltpu.make_async_copy(
            gains.at[level, targets(level)[place]], factors.at[level, place], gain_sem
        )

    def exchange(level, chunk, size):
        if level == 0:
            source = coefs.at[1 - sides[0], part(chunk, size)]
        else:
            source = given.at[level - 1, part(chunk, size)]
        return pltpu.make_async_remote_copy(
            src_ref=source,
            dst_ref=passing.at[part(chunk, size)] if level == 2 else arrived.at[level, part(chunk, size)],
            send_sem=send_sems.at[level],
            recv_sem=pass_sems.at[chunk] if level == 2 else recv_sems.at[level, chunk],
            device_id=partners[level],
            device_id_type=MESH,
        )

    def onward(chunk, size):
        return pltpu.make_async_remote_copy(
            src_ref=passing.at[part(chunk, size)],
            dst_ref=arrived.at[2, part(chunk, size)],
            send_sem=send_sems.at[LEVELS],
            recv_sem=recv_sems.at[2, chunk],
            device_id=partners[2],
            device_id_type=MESH,
        )

    own_copy = pltpu.make_async_copy(coefs.at[sides[0]], own, own_sem)
    block_copy = pltpu.make_async_copy(blocks, blocks_in, block_sem)
    block_copy.start()
    own_copy.start()
    for level in range(LEVELS):
        for place in range(2):
            load_gains(level, place).start()

    barrier = pltpu.get_barrier_semaphore()
    for peer in (partners[0], {"gz": (gz + 1) % 4}, {"gz": (gz + 3) % 4}, partners[3]):
        pl.semaphore_signal(barrier, inc=1, device_id=peer, device_id_type=MESH)
    pl.semaphore_wait(barrier, 4)

    for chunk in range(FIRST):
        exchange(0, chunk, SMALL if chunk < HEAD else LARGE).start()

    block_copy.wait()
    for level in range(LEVELS):
        for place in range(2):
            for origin in range(2):
                source = sides[level] if origin == 0 else 1 - sides[level]
                weights[level, pl.ds(origin * width, width), pl.ds(place * width, width)] = blocks_in[
                    level, targets(level)[place], source
                ]
    pltpu.make_async_copy(factors, factors, gain_sem).wait()
    own_copy.wait()

    def work(level, chunk, size):
        here = part(chunk, size)
        rows = size * vecs
        if level == 0:
            self_rows = own
        else:
            self_rows = kept.at[level - 1]
        if level == 2:
            onward(chunk, size).wait_recv()
        else:
            exchange(level, chunk, size).wait_recv()
        joined = jnp.concatenate(
            [self_rows[here].reshape(rows, width), arrived[level, here].reshape(rows, width)], axis=1
        )
        total = jnp.dot(joined, weights[level], preferred_element_type=jnp.float32)
        for place in range(2):
            scale = factors[level, place, here].astype(jnp.float32)
            columns = total[:, place * width : (place + 1) * width].reshape(size, vecs, width)
            values = (columns * scale[:, None, :]).astype(jnp.bfloat16)
            if level == LEVELS - 1:
                result[place, here] = values
            elif place == 0:
                given[level, here] = values
                exchange(level + 1, chunk, size).start()
            else:
                kept[level, here] = values

    def forward(chunk, size):
        exchange(2, chunk, size).wait_recv()
        onward(chunk, size).start()

    def when_valid(chunk, action):
        @pl.when((chunk >= 0) & (chunk < chunks))
        def _():
            by_size(chunk, action)

    def begin(chunk, size):
        exchange(0, chunk, size).start()

    def step(index, carry):
        when_valid(index, functools.partial(work, 0))
        if FIRST < AHEAD + 1:

            @pl.when(index == 0)
            def _():
                for chunk in range(FIRST, AHEAD):
                    begin(chunk, SMALL if chunk < HEAD else LARGE)

        when_valid(index + AHEAD, begin)
        when_valid(index - LAGS[1], functools.partial(work, 1))
        when_valid(index - PASS_LAG, forward)
        when_valid(index - LAGS[2], functools.partial(work, 2))
        when_valid(index - LAGS[3], functools.partial(work, 3))
        return carry

    lax.fori_loop(0, chunks + LAGS[-1], step, 0)

    for index in range(LEVELS + 1):
        pltpu.make_async_copy(arrived.at[0], arrived.at[0], send_sems.at[index]).wait()


def in_hbm(array):
    return pltpu.with_memory_space_constraint(array, pltpu.HBM)


def shards(coefficients, translations, box_gains):
    boxes, vecs, width = coefficients.shape
    half = boxes // 2
    chunks = (half - (HEAD + TAIL) * SMALL) // LARGE + HEAD + TAIL
    bf16 = jnp.bfloat16
    anywhere = pl.BlockSpec(memory_space=pltpu.HBM)
    result = pl.pallas_call(
        butterfly,
        out_shape=pltpu.VMEM((2, half, vecs, width), bf16),
        in_specs=[anywhere] * 3,
        out_specs=pl.BlockSpec(memory_space=pltpu.VMEM),
        scratch_shapes=[
            pltpu.VMEM((half, vecs, width), bf16),
            pltpu.VMEM(translations.shape, bf16),
            pltpu.VMEM((LEVELS, 2 * width, 2 * width), bf16),
            pltpu.VMEM((LEVELS, 2, half, width), bf16),
            pltpu.VMEM((LEVELS - 1, half, vecs, width), bf16),
            pltpu.VMEM((LEVELS - 1, half, vecs, width), bf16),
            pltpu.VMEM((LEVELS, half, vecs, width), bf16),
            pltpu.VMEM((half, vecs, width), bf16),
            pltpu.SemaphoreType.DMA,
            pltpu.SemaphoreType.DMA,
            pltpu.SemaphoreType.DMA,
            pltpu.SemaphoreType.DMA((LEVELS + 1,)),
            pltpu.SemaphoreType.DMA((LEVELS, chunks)),
            pltpu.SemaphoreType.DMA((chunks,)),
        ],
        compiler_params=pltpu.CompilerParams(
            collective_id=0, has_side_effects=True, vmem_limit_bytes=48 * 2**20
        ),
        cost_estimate=pl.CostEstimate(
            flops=LEVELS * 2 * half * vecs * 4 * width * width,
            bytes_accessed=10 * 2**20,
            transcendentals=0,
        ),
    )(
        in_hbm(coefficients.reshape(2, half, vecs, width)),
        in_hbm(translations),
        in_hbm(box_gains.reshape(LEVELS, 2, half, width)),
    )
    return result.reshape(boxes, vecs, width)


def solution(mesh):
    return jax.shard_map(
        shards,
        mesh=mesh,
        in_specs=(P(("gx", "gy", "gz"), None, None), P(), P(None, ("gx", "gy", "gz"), None)),
        out_specs=P(("gx", "gy", "gz"), None, None),
        check_vma=False,
    )
```

```python
import functools

import jax
import jax.numpy as jnp
from jax import lax
from jax.experimental import pallas as pl
from jax.experimental.pallas import tpu as pltpu
from jax.sharding import PartitionSpec as P

MESH = pl.DeviceIdType.MESH
LEVELS = 4
SMALL = 16
LARGE = 32
HEAD = 6
TAIL = 2
FIRST = 2
AHEAD = 3
REUSE = 8
LAGS = (0, 2, 9, 11)
PASS_LAG = 5


def butterfly(
    coefs, blocks, gains, result,
    own, blocks_in, weights, factors, kept, given, arrived, passing,
    own_sem, block_sem, gain_sem, send_sems, recv_sems, pass_sems,
):
    gx, gy, gz = lax.axis_index("gx"), lax.axis_index("gy"), lax.axis_index("gz")
    sides = (gx % 2, gz % 2, gz // 2, gy % 2)
    partners = (
        {"gx": gx + 1 - 2 * sides[0]},
        {"gz": gz + 1 - 2 * sides[1]},
        {"gz": (gz + 1 + 2 * sides[3]) % 4},
        {"gy": gy + 1 - 2 * sides[3]},
    )
    half, vecs, width = own.shape
    larges = (half - (HEAD + TAIL) * SMALL) // LARGE
    chunks = larges + HEAD + TAIL

    def part(chunk, size):
        if size == LARGE:
            return pl.ds((chunk - HEAD) * LARGE + HEAD * SMALL, LARGE)
        late = (chunk + chunks - larges - HEAD) // chunks
        return pl.ds(chunk * SMALL + late * larges * (LARGE - SMALL), SMALL)

    def by_size(chunk, action):
        inner = (chunk >= HEAD) & (chunk < HEAD + larges)

        @pl.when(inner)
        def _():
            action(chunk, LARGE)

        @pl.when(jnp.logical_not(inner))
        def _():
            action(chunk, SMALL)

    def targets(level):
        if level == LEVELS - 1:
            return (0, 1)
        return (1 - sides[level + 1], sides[level + 1])

    def load_gains(level, place):
        return pltpu.make_async_copy(
            gains.at[level, targets(level)[place]], factors.at[level, place], gain_sem
        )

    def exchange(level, chunk, size):
        if level == 0:
            source = coefs.at[1 - sides[0], part(chunk, size)]
        else:
            source = given.at[level - 1, part(chunk, size)]
        return pltpu.make_async_remote_copy(
            src_ref=source,
            dst_ref=passing.at[part(chunk, size)] if level == 2 else arrived.at[level, part(chunk, size)],
            send_sem=send_sems.at[level],
            recv_sem=pass_sems.at[0, chunk] if level == 2 else recv_sems.at[level - level // 3, chunk % REUSE],
            device_id=partners[level],
            device_id_type=MESH,
        )

    def onward(chunk, size):
        return pltpu.make_async_remote_copy(
            src_ref=passing.at[part(chunk, size)],
            dst_ref=arrived.at[2, part(chunk, size)],
            send_sem=send_sems.at[LEVELS],
            recv_sem=pass_sems.at[1, chunk],
            device_id=partners[2],
            device_id_type=MESH,
        )

    own_copy = pltpu.make_async_copy(coefs.at[sides[0]], own, own_sem)
    block_copy = pltpu.make_async_copy(blocks, blocks_in, block_sem)
    block_copy.start()
    own_copy.start()
    for level in range(LEVELS):
        for place in range(2):
            load_gains(level, place).start()

    barrier = pltpu.get_barrier_semaphore()
    for peer in (partners[0], {"gz": (gz + 1) % 4}, {"gz": (gz + 3) % 4}, partners[3]):
        pl.semaphore_signal(barrier, inc=1, device_id=peer, device_id_type=MESH)
    pl.semaphore_wait(barrier, 4)

    for chunk in range(FIRST):
        exchange(0, chunk, SMALL if chunk < HEAD else LARGE).start()

    block_copy.wait()
    for level in range(LEVELS):
        for place in range(2):
            for origin in range(2):
                source = sides[level] if origin == 0 else 1 - sides[level]
                weights[level, pl.ds(origin * width, width), pl.ds(place * width, width)] = blocks_in[
                    level, targets(level)[place], source
                ]
    pltpu.make_async_copy(factors, factors, gain_sem).wait()
    own_copy.wait()

    def work(level, chunk, size):
        here = part(chunk, size)
        rows = size * vecs
        if level == 0:
            self_rows = own
        else:
            self_rows = kept.at[level - 1]
        if level == 2:
            onward(chunk, size).wait_recv()
        else:
            exchange(level, chunk, size).wait_recv()
        joined = jnp.concatenate(
            [self_rows[here].reshape(rows, width), arrived[level, here].reshape(rows, width)], axis=1
        )
        total = jnp.dot(joined, weights[level], preferred_element_type=jnp.float32)
        for place in range(2):
            scale = factors[level, place, here].astype(jnp.float32)
            columns = total[:, place * width : (place + 1) * width].reshape(size, vecs, width)
            values = (columns * scale[:, None, :]).astype(jnp.bfloat16)
            if level == LEVELS - 1:
                result[place, here] = values
            elif place == 0:
                given[level, here] = values
                exchange(level + 1, chunk, size).start()
            else:
                kept[level, here] = values

    def forward(chunk, size):
        exchange(2, chunk, size).wait_recv()
        onward(chunk, size).start()

    def when_valid(chunk, action):
        @pl.when((chunk >= 0) & (chunk < chunks))
        def _():
            by_size(chunk, action)

    def begin(chunk, size):
        exchange(0, chunk, size).start()

    def step(index, carry):
        when_valid(index, functools.partial(work, 0))
        if FIRST < AHEAD + 1:

            @pl.when(index == 0)
            def _():
                for chunk in range(FIRST, AHEAD):
                    begin(chunk, SMALL if chunk < HEAD else LARGE)

        when_valid(index + AHEAD, begin)
        when_valid(index - LAGS[1], functools.partial(work, 1))
        when_valid(index - PASS_LAG, forward)
        when_valid(index - LAGS[2], functools.partial(work, 2))
        when_valid(index - LAGS[3], functools.partial(work, 3))
        return carry

    lax.fori_loop(0, chunks + LAGS[-1], step, 0)

    for index in range(LEVELS + 1):
        pltpu.make_async_copy(arrived.at[0], arrived.at[0], send_sems.at[index]).wait()


def in_hbm(array):
    return pltpu.with_memory_space_constraint(array, pltpu.HBM)


def shards(coefficients, translations, box_gains):
    boxes, vecs, width = coefficients.shape
    half = boxes // 2
    chunks = (half - (HEAD + TAIL) * SMALL) // LARGE + HEAD + TAIL
    bf16 = jnp.bfloat16
    anywhere = pl.BlockSpec(memory_space=pltpu.HBM)
    result = pl.pallas_call(
        butterfly,
        out_shape=pltpu.VMEM((2, half, vecs, width), bf16),
        in_specs=[anywhere] * 3,
        out_specs=pl.BlockSpec(memory_space=pltpu.VMEM),
        scratch_shapes=[
            pltpu.VMEM((half, vecs, width), bf16),
            pltpu.VMEM(translations.shape, bf16),
            pltpu.VMEM((LEVELS, 2 * width, 2 * width), bf16),
            pltpu.VMEM((LEVELS, 2, half, width), bf16),
            pltpu.VMEM((LEVELS - 1, half, vecs, width), bf16),
            pltpu.VMEM((LEVELS - 1, half, vecs, width), bf16),
            pltpu.VMEM((LEVELS, half, vecs, width), bf16),
            pltpu.VMEM((half, vecs, width), bf16),
            pltpu.SemaphoreType.DMA,
            pltpu.SemaphoreType.DMA,
            pltpu.SemaphoreType.DMA,
            pltpu.SemaphoreType.DMA((LEVELS + 1,)),
            pltpu.SemaphoreType.DMA((LEVELS - 1, REUSE)),
            pltpu.SemaphoreType.DMA((2, chunks)),
        ],
        compiler_params=pltpu.CompilerParams(
            collective_id=0, has_side_effects=True, vmem_limit_bytes=48 * 2**20
        ),
        cost_estimate=pl.CostEstimate(
            flops=LEVELS * 2 * half * vecs * 4 * width * width,
            bytes_accessed=10 * 2**20,
            transcendentals=0,
        ),
    )(
        in_hbm(coefficients.reshape(2, half, vecs, width)),
        in_hbm(translations),
        in_hbm(box_gains.reshape(LEVELS, 2, half, width)),
    )
    return result.reshape(boxes, vecs, width)


def solution(mesh):
    return jax.shard_map(
        shards,
        mesh=mesh,
        in_specs=(P(("gx", "gy", "gz"), None, None), P(), P(None, ("gx", "gy", "gz"), None)),
        out_specs=P(("gx", "gy", "gz"), None, None),
        check_vma=False,
    )
```

```python
import functools

import jax
import jax.numpy as jnp
from jax import lax
from jax.experimental import pallas as pl
from jax.experimental.pallas import tpu as pltpu
from jax.sharding import PartitionSpec as P

MESH = pl.DeviceIdType.MESH
LEVELS = 4
SMALL = 16
LARGE = 32
HEAD = 6
TAIL = 2
FIRST = 2
AHEAD = 2
REUSE = 8
LAGS = (0, 2, 9, 11)
PASS_LAG = 5


def butterfly(
    coefs, blocks, gains, result,
    own, blocks_in, weights, factors, kept, given, arrived, passing,
    own_sem, block_sem, gain_sem, send_sems, recv_sems, pass_sems,
):
    gx, gy, gz = lax.axis_index("gx"), lax.axis_index("gy"), lax.axis_index("gz")
    sides = (gx % 2, gz % 2, gz // 2, gy % 2)

    def along(steps):
        place = (2 * gz + sides[0] + steps) % 8
        return {"gx": gx - sides[0] + place % 2, "gz": place // 2}

    partners = (
        {"gx": gx + 1 - 2 * sides[0]},
        {"gz": gz + 1 - 2 * sides[1]},
        along(3 * (1 + 6 * sides[3])),
        {"gy": gy + 1 - 2 * sides[3]},
    )
    half, vecs, width = own.shape
    larges = (half - (HEAD + TAIL) * SMALL) // LARGE
    chunks = larges + HEAD + TAIL

    def part(chunk, size):
        if size == LARGE:
            return pl.ds((chunk - HEAD) * LARGE + HEAD * SMALL, LARGE)
        late = (chunk + chunks - larges - HEAD) // chunks
        return pl.ds(chunk * SMALL + late * larges * (LARGE - SMALL), SMALL)

    def by_size(chunk, action):
        inner = (chunk >= HEAD) & (chunk < HEAD + larges)

        @pl.when(inner)
        def _():
            action(chunk, LARGE)

        @pl.when(jnp.logical_not(inner))
        def _():
            action(chunk, SMALL)

    def targets(level):
        if level == LEVELS - 1:
            return (0, 1)
        return (1 - sides[level + 1], sides[level + 1])

    def load_gains(level, place):
        return pltpu.make_async_copy(
            gains.at[level, targets(level)[place]], factors.at[level, place], gain_sem
        )

    def exchange(level, chunk, size):
        if level == 0:
            source = coefs.at[1 - sides[0], part(chunk, size)]
        else:
            source = given.at[level - 1, part(chunk, size)]
        return pltpu.make_async_remote_copy(
            src_ref=source,
            dst_ref=passing.at[part(chunk, size)] if level == 2 else arrived.at[level, part(chunk, size)],
            send_sem=send_sems.at[level],
            recv_sem=pass_sems.at[0, chunk] if level == 2 else recv_sems.at[level - level // 3, chunk % REUSE],
            device_id=partners[level],
            device_id_type=MESH,
        )

    def onward(chunk, size):
        return pltpu.make_async_remote_copy(
            src_ref=passing.at[part(chunk, size)],
            dst_ref=arrived.at[2, part(chunk, size)],
            send_sem=send_sems.at[LEVELS],
            recv_sem=pass_sems.at[1, chunk],
            device_id=along(1 + 6 * sides[3]),
            device_id_type=MESH,
        )

    own_copy = pltpu.make_async_copy(coefs.at[sides[0]], own, own_sem)
    block_copy = pltpu.make_async_copy(blocks, blocks_in, block_sem)
    block_copy.start()
    own_copy.start()
    for level in range(LEVELS):
        for place in range(2):
            load_gains(level, place).start()

    barrier = pltpu.get_barrier_semaphore()
    for peer in (along(1), along(3), along(5), along(7), partners[1], partners[3]):
        pl.semaphore_signal(barrier, inc=1, device_id=peer, device_id_type=MESH)
    pl.semaphore_wait(barrier, 6)

    for chunk in range(FIRST):
        exchange(0, chunk, SMALL if chunk < HEAD else LARGE).start()

    block_copy.wait()
    for level in range(LEVELS):
        for place in range(2):
            for origin in range(2):
                source = sides[level] if origin == 0 else 1 - sides[level]
                weights[level, pl.ds(origin * width, width), pl.ds(place * width, width)] = blocks_in[
                    level, targets(level)[place], source
                ]
    pltpu.make_async_copy(factors, factors, gain_sem).wait()
    own_copy.wait()

    def work(level, chunk, size):
        here = part(chunk, size)
        rows = size * vecs
        if level == 0:
            self_rows = own
        else:
            self_rows = kept.at[level - 1]
        if level == 2:
            onward(chunk, size).wait_recv()
        else:
            exchange(level, chunk, size).wait_recv()
        joined = jnp.concatenate(
            [self_rows[here].reshape(rows, width), arrived[level, here].reshape(rows, width)], axis=1
        )
        total = jnp.dot(joined, weights[level], preferred_element_type=jnp.float32)
        for place in range(2):
            scale = factors[level, place, here].astype(jnp.float32)
            columns = total[:, place * width : (place + 1) * width].reshape(size, vecs, width)
            values = (columns * scale[:, None, :]).astype(jnp.bfloat16)
            if level == LEVELS - 1:
                result[place, here] = values
            elif place == 0:
                given[level, here] = values
                exchange(level + 1, chunk, size).start()
            else:
                kept[level, here] = values

    def forward(chunk, size):
        exchange(2, chunk, size).wait_recv()
        onward(chunk, size).start()

    def when_valid(chunk, action):
        @pl.when((chunk >= 0) & (chunk < chunks))
        def _():
            by_size(chunk, action)

    def begin(chunk, size):
        exchange(0, chunk, size).start()

    def step(index, carry):
        when_valid(index, functools.partial(work, 0))
        if FIRST < AHEAD + 1:

            @pl.when(index == 0)
            def _():
                for chunk in range(FIRST, AHEAD):
                    begin(chunk, SMALL if chunk < HEAD else LARGE)

        when_valid(index + AHEAD, begin)
        when_valid(index - LAGS[1], functools.partial(work, 1))
        when_valid(index - PASS_LAG, forward)
        when_valid(index - LAGS[2], functools.partial(work, 2))
        when_valid(index - LAGS[3], functools.partial(work, 3))
        return carry

    lax.fori_loop(0, chunks + LAGS[-1], step, 0)

    for index in range(LEVELS + 1):
        pltpu.make_async_copy(arrived.at[0], arrived.at[0], send_sems.at[index]).wait()


def in_hbm(array):
    return pltpu.with_memory_space_constraint(array, pltpu.HBM)


def shards(coefficients, translations, box_gains):
    boxes, vecs, width = coefficients.shape
    half = boxes // 2
    chunks = (half - (HEAD + TAIL) * SMALL) // LARGE + HEAD + TAIL
    bf16 = jnp.bfloat16
    anywhere = pl.BlockSpec(memory_space=pltpu.HBM)
    result = pl.pallas_call(
        butterfly,
        out_shape=pltpu.VMEM((2, half, vecs, width), bf16),
        in_specs=[anywhere] * 3,
        out_specs=pl.BlockSpec(memory_space=pltpu.VMEM),
        scratch_shapes=[
            pltpu.VMEM((half, vecs, width), bf16),
            pltpu.VMEM(translations.shape, bf16),
            pltpu.VMEM((LEVELS, 2 * width, 2 * width), bf16),
            pltpu.VMEM((LEVELS, 2, half, width), bf16),
            pltpu.VMEM((LEVELS - 1, half, vecs, width), bf16),
            pltpu.VMEM((LEVELS - 1, half, vecs, width), bf16),
            pltpu.VMEM((LEVELS, half, vecs, width), bf16),
            pltpu.VMEM((half, vecs, width), bf16),
            pltpu.SemaphoreType.DMA,
            pltpu.SemaphoreType.DMA,
            pltpu.SemaphoreType.DMA,
            pltpu.SemaphoreType.DMA((LEVELS + 1,)),
            pltpu.SemaphoreType.DMA((LEVELS - 1, REUSE)),
            pltpu.SemaphoreType.DMA((2, chunks)),
        ],
        compiler_params=pltpu.CompilerParams(
            collective_id=0, has_side_effects=True, vmem_limit_bytes=48 * 2**20
        ),
        cost_estimate=pl.CostEstimate(
            flops=LEVELS * 2 * half * vecs * 4 * width * width,
            bytes_accessed=10 * 2**20,
            transcendentals=0,
        ),
    )(
        in_hbm(coefficients.reshape(2, half, vecs, width)),
        in_hbm(translations),
        in_hbm(box_gains.reshape(LEVELS, 2, half, width)),
    )
    return result.reshape(boxes, vecs, width)


def solution(mesh):
    return jax.shard_map(
        shards,
        mesh=mesh,
        in_specs=(P(("gx", "gy", "gz"), None, None), P(), P(None, ("gx", "gy", "gz"), None)),
        out_specs=P(("gx", "gy", "gz"), None, None),
        check_vma=False,
    )
```
